32 devices in a mesh: grp: 2 (over x), ex: 16 (over z, y, core).
Axes of the slice: x: 2, y: 2, z: 4, core: 2. Of those that a mesh axis runs over, the one named last changes fastest.
Arguments:
- train_grads: bfloat16 [12288, 16384], P(('grp', 'ex')), parts along dimension 0, may hold values from -100 to 100
- queries: bfloat16 [2, 1024, 16384], P(None, ('grp', 'ex')), parts along dimension 1, may hold values from -6 to 6
- left_factor: bfloat16 [4, 64, 64], replicated, may hold values from -0.5 to 1.5
- right_factor: bfloat16 [4, 64, 64], replicated, may hold values from -0.5 to 1.5
Outputs:
- scores: float32 [12288, 1024], P(('grp', 'ex')), parts along dimension 0
The draws below stay inside these ranges and needn't reach their ends.
There are 2 independent parts, one for each index of `grp`. The reference program is written for one: setup_inputs(seed, part) draws one part's arguments, and reference() takes and returns one part's arrays. A program takes and returns all parts, laid end to end along the dimension named above; an argument that names none is the same for every part. Nothing has to cross between parts.
All inputs are finite; a program needn't handle non-finite values.
Results may differ from the reference program's by a relative error of at most 0.0043.
Values may be sent and summed in bfloat16 or wider, within the bound.
A program may use at most 192 MiB of HBM per device.

```python
import math
import jax
import jax.numpy as jnp
from jax import lax

F = 16384
KIN = 64
KOUT = 64
MODULES = 4
QBLOCK = 512
TRAIN = 6144


def factor_draw(key, width):
    perturb = jnp.clip(jax.random.normal(key, (MODULES, width, width), jnp.float32), -4.0, 4.0)
    return jnp.eye(width, dtype=jnp.float32)[None] + 0.125 * perturb


def draw_left_factor(key, part):
    key = jax.random.fold_in(key, 11)
    return factor_draw(key, KIN).astype(jnp.bfloat16)


def draw_right_factor(key, part):
    key = jax.random.fold_in(key, 17)
    return factor_draw(key, KOUT).astype(jnp.bfloat16)


def draw_train_grads(key, part):
    key = jax.random.fold_in(key, 23)
    key_scale, key_body = jax.random.split(key, 2)
    position = jnp.arange(TRAIN, dtype=jnp.float32) / TRAIN
    spread = jnp.exp(jax.random.uniform(key_scale, (TRAIN,), jnp.float32) * math.log(10.0))
    growth = jnp.exp(position * math.log(3.0))
    normal_part = jnp.clip(jax.random.normal(key_body, (TRAIN, F), jnp.float32), -5.0, 5.0)
    return (0.3 * normal_part * (spread * growth)[:, None]).astype(jnp.bfloat16)


def shard_levels(rng, dims, cuts, low, largest):
    def one(axis_at, shards_of):
        steps = jax.random.uniform(jax.random.fold_in(jax.random.fold_in(rng, 6), axis_at), (shards_of,), jnp.float32, low / len(cuts), largest / len(cuts))
        return jnp.repeat(jnp.exp(steps), dims[axis_at] // shards_of).reshape((-1,) + (1,) * (len(dims) - axis_at - 1))

    factor_of = one(*cuts[0])
    for cut in cuts[1:]:
        factor_of = factor_of * one(*cut)
    return factor_of


def scatter_about(own_key, shape, deviation, reach, shards=(), held_as=jnp.bfloat16):
    array = deviation * jax.random.normal(own_key, shape, jnp.float32)
    if shards:
        array = array * shard_levels(own_key, shape, shards, -0.22, 0.18)
    return jnp.clip(array, -reach, reach).astype(held_as)


def setup_inputs(seed: int = 0, part: int = 0) -> dict:
    splits = jax.random.split(jax.random.key(seed), 5)
    part_keys = jax.random.split(jax.random.fold_in(splits[4], part), 5)
    return {
        "train_grads": draw_train_grads(jax.random.fold_in(jax.random.fold_in(splits[4], part), 71), part),
        "queries": scatter_about(part_keys[1], (2, QBLOCK, F), 1.0, 6.0, ((1, 16),)),
        "left_factor": draw_left_factor(jax.random.fold_in(splits[4], 71), part),
        "right_factor": draw_right_factor(jax.random.fold_in(splits[4], 71), part),
    }


def condition(gradients, left_factor, right_factor):
    modules, inner, _ = left_factor.shape
    outer = right_factor.shape[1]
    leading = gradients.shape[:-1]
    blocks_view = gradients.astype(jnp.float32).reshape(leading + (modules, inner, outer))
    halfway = jnp.einsum('mij,...mjk->...mik', left_factor.astype(jnp.float32), blocks_view, precision=lax.Precision.HIGHEST)
    halfway = halfway.astype(jnp.bfloat16).astype(jnp.float32)
    full = jnp.einsum('...mik,mkl->...mil', halfway, right_factor.astype(jnp.float32), precision=lax.Precision.HIGHEST)
    return full.reshape(leading + (modules * inner * outer,)).astype(jnp.bfloat16)

def reference(train_grads, queries, left_factor, right_factor):
    prepared = condition(queries, left_factor, right_factor)
    flat_queries = prepared.reshape(-1, prepared.shape[-1])
    raw_scores = jnp.dot(train_grads, flat_queries.T, preferred_element_type=jnp.float32)
    squares = lax.optimization_barrier(jnp.sum(raw_scores * raw_scores, axis=0))
    inverse_rms = lax.rsqrt(squares / TRAIN + 1e-06)
    return raw_scores * inverse_rms[None, :]
```

```python
import functools

import jax
import jax.numpy as jnp
from jax import lax
from jax.experimental import pallas as pl
from jax.experimental.pallas import tpu as pltpu
from jax.sharding import PartitionSpec as P

PARTS = 4


def condition(gradients, left_factor, right_factor):
    modules, inner, _ = left_factor.shape
    outer = right_factor.shape[1]
    leading = gradients.shape[:-1]
    blocks_view = gradients.reshape(leading + (modules, inner, outer))
    halfway = jnp.einsum(
        "mij,...mjk->...mik", left_factor, blocks_view, preferred_element_type=jnp.float32
    )
    halfway = halfway.astype(jnp.bfloat16)
    full = jnp.einsum(
        "...mik,mkl->...mil", halfway, right_factor, preferred_element_type=jnp.float32
    )
    return full.reshape(leading + (modules * inner * outer,)).astype(jnp.bfloat16)


def ring_kernel(
    size, prepared_ref, train_ref, scores_ref, squares_ref,
    held, train, acc, flipped, mine, sums,
    own_sem, train_sem, send_sem, recv_sem, twin_send, twin_recv, sum_send, sum_recv,
):
    chips = size // 2
    rows = prepared_ref.shape[1]
    width = prepared_ref.shape[2] // PARTS
    block = size * rows
    me = lax.axis_index("ex")
    place, core = me // 2, lax.rem(me, 2)
    twin = place * 2 + 1 - core
    snake = size == 16

    def place_of(at):
        if not snake:
            return at
        side = at // (chips // 2)
        return 2 * (at + side * (chips - 1 - 2 * at)) + side

    at = place
    if snake:
        side, high = lax.rem(place, 2), place // 2
        at = high + side * (chips - 1 - 2 * high)
    ahead = place_of(lax.rem(at + 1, chips)) * 2 + core
    behind = place_of(lax.rem(at + chips - 1, chips)) * 2 + core

    def part(index):
        return pl.ds(index * width, width)

    def own_copy(way, index):
        return pltpu.make_async_copy(
            prepared_ref.at[way, :, part(index)],
            held.at[way, pl.ds(pl.multiple_of(me * rows, rows), rows), part(index)],
            own_sem.at[way, index],
        )

    def train_copy(index):
        return pltpu.make_async_copy(
            train_ref.at[:, part(index)], train.at[:, part(index)], train_sem.at[index]
        )

    for index in range(PARTS):
        for way in range(2):
            own_copy(way, index).start()
    for index in range(PARTS):
        train_copy(index).start()

    barrier = pltpu.get_barrier_semaphore()

    @pl.loop(1, size)
    def _(shift):
        pl.semaphore_signal(
            barrier, inc=1, device_id={"ex": lax.rem(me + shift, size)},
            device_id_type=pl.DeviceIdType.MESH,
        )

    pl.semaphore_wait(barrier, size - 1)

    def source(way, step):
        return place_of(lax.rem(at + (chips - step if way == 0 else step), chips))

    def slot(way, step, whose, index):
        start = (source(way, step) * 2 + whose) * rows
        return held.at[way, pl.ds(pl.multiple_of(start, rows), rows), part(index)]

    def forward(way, step, index):
        view = slot(way, step, core, index)
        return pltpu.make_async_remote_copy(
            src_ref=view, dst_ref=view,
            send_sem=send_sem.at[way, index], recv_sem=recv_sem.at[way, step, index],
            device_id={"ex": ahead if way == 0 else behind},
            device_id_type=pl.DeviceIdType.MESH,
        )

    def share(way, step, index):
        view = slot(way, step, core, index)
        return pltpu.make_async_remote_copy(
            src_ref=view, dst_ref=view,
            send_sem=twin_send.at[way, index], recv_sem=twin_recv.at[way, step, index],
            device_id={"ex": twin}, device_id_type=pl.DeviceIdType.MESH,
        )

    def arrived(way, step, whose, index, sem):
        view = slot(way, step, whose, index)
        pltpu.make_async_copy(view, view, sem).wait()

    @pl.loop(0, chips)
    def _(step):
        for index in range(PARTS):
            for way in range(2):
                @pl.when(step == 0)
                def _():
                    own_copy(way, index).wait()

                @pl.when(step > 0)
                def _():
                    arrived(way, step, core, index, recv_sem.at[way, step - 1, index])
                    forward(way, step - 1, index).wait_send()

                @pl.when(step < chips - 1)
                def _():
                    forward(way, step, index).start()

                @pl.when(step > 0)
                def _():
                    share(way, step - 1, index).wait_send()

                share(way, step, index).start()

            @pl.when(step == 0)
            def _():
                train_copy(index).wait()

            for way in range(2):
                arrived(way, step, 1 - core, index, twin_recv.at[way, step, index])
            pair = [
                held[way, pl.ds(pl.multiple_of(source(way, step) * 2 * rows, 2 * rows), 2 * rows), part(index)]
                for way in range(2)
            ]
            product = lax.dot_general(
                train[:, part(index)], jnp.concatenate(pair, axis=0),
                (((1,), (1,)), ((), ())), preferred_element_type=jnp.float32,
            )
            if index == 0:
                acc[...] = product
            elif index < PARTS - 1:
                acc[...] += product
            else:
                turned = (acc[...] + product).T
                for way in range(2):
                    start = way * block + source(way, step) * 2 * rows
                    flipped[pl.ds(pl.multiple_of(start, 2 * rows), 2 * rows), :] = turned[
                        way * 2 * rows : (way + 1) * 2 * rows
                    ]

    for index in range(PARTS):
        for way in range(2):
            share(way, chips - 1, index).wait_send()

    for start in range(0, 2 * block, 128):
        columns = flipped[start : start + 128, :].T
        scores_ref[:, start : start + 128] = columns
        mine[:, start : start + 128] = jnp.sum(columns * columns, axis=0, keepdims=True)

    def tell(shift):
        return pltpu.make_async_remote_copy(
            src_ref=mine, dst_ref=sums.at[shift],
            send_sem=sum_send.at[shift], recv_sem=sum_recv.at[shift],
            device_id={"ex": lax.rem(me + shift, size)},
            device_id_type=pl.DeviceIdType.MESH,
        )

    @pl.loop(1, size)
    def _(shift):
        tell(shift).start()

    sums[0] = mine[...]

    @pl.loop(1, size)
    def _(shift):
        tell(shift).wait()

    squares_ref[...] = jnp.sum(sums[...], axis=0)


def on_device(train_grads, queries, left_factor, right_factor):
    size = lax.axis_size("ex")
    count, features = train_grads.shape
    train_count = count * size
    prepared = condition(queries, left_factor, right_factor)
    blocks, rows, _ = queries.shape
    columns = blocks * size * rows
    chips = size // 2
    raw_scores, squares = pl.pallas_call(
        functools.partial(ring_kernel, size),
        out_shape=(
            jax.ShapeDtypeStruct((count, columns), jnp.float32),
            jax.ShapeDtypeStruct((1, columns), jnp.float32),
        ),
        in_specs=[pl.BlockSpec(memory_space=pl.ANY)] * 2,
        out_specs=(pl.BlockSpec(memory_space=pltpu.VMEM),) * 2,
        scratch_shapes=[
            pltpu.VMEM((2, size * rows, features), jnp.bfloat16),
            pltpu.VMEM((count, features), jnp.bfloat16),
            pltpu.VMEM((count, 4 * rows), jnp.float32),
            pltpu.VMEM((columns, count), jnp.float32),
            pltpu.VMEM((1, columns), jnp.float32),
            pltpu.VMEM((size, 1, columns), jnp.float32),
            pltpu.SemaphoreType.DMA((2, PARTS)),
            pltpu.SemaphoreType.DMA((PARTS,)),
            pltpu.SemaphoreType.DMA((2, PARTS)),
            pltpu.SemaphoreType.DMA((2, chips - 1, PARTS)),
            pltpu.SemaphoreType.DMA((2, PARTS)),
            pltpu.SemaphoreType.DMA((2, chips, PARTS)),
            pltpu.SemaphoreType.DMA((size,)),
            pltpu.SemaphoreType.DMA((size,)),
        ],
        compiler_params=pltpu.CompilerParams(
            collective_id=0, has_side_effects=True, vmem_limit_bytes=58 * 1024 * 1024
        ),
        cost_estimate=pl.CostEstimate(
            flops=2 * count * columns * features,
            bytes_accessed=2 * count * features + 4 * count * columns,
            transcendentals=0,
        ),
    )(prepared, train_grads)
    inverse_rms = lax.rsqrt(squares / train_count + 1e-06)
    return raw_scores * inverse_rms


def solution(mesh):
    in_specs = (P(("grp", "ex"), None), P(None, ("grp", "ex"), None), P(), P())
    out_specs = P(("grp", "ex"), None)
    return jax.shard_map(
        on_device, mesh=mesh, in_specs=in_specs, out_specs=out_specs, check_vma=False
    )
```

```python
import functools

import jax
import jax.numpy as jnp
from jax import lax
from jax.experimental import pallas as pl
from jax.experimental.pallas import tpu as pltpu
from jax.sharding import PartitionSpec as P

LANES = 128


def spread_left(left):
    inner = left.shape[0]
    half = inner // 2
    at = lax.broadcasted_iota(jnp.int32, (inner, inner), 0)
    of = lax.broadcasted_iota(jnp.int32, (inner, inner), 1)
    move = (of == jnp.where(at < half, 2 * at, 2 * (at - half) + 1)).astype(jnp.float32).astype(jnp.bfloat16)
    back = (at == jnp.where(of < half, 2 * of, 2 * (of - half) + 1)).astype(jnp.float32).astype(jnp.bfloat16)
    rows_moved = jnp.dot(move, left, preferred_element_type=jnp.float32).astype(jnp.bfloat16)
    return jnp.dot(rows_moved, back, preferred_element_type=jnp.float32).astype(jnp.bfloat16)


def spread_right(right):
    outer = right.shape[0]
    full = 4 * outer
    tall = lax.broadcasted_iota(jnp.int32, (full, outer), 0) & (outer - 1)
    down = (tall == lax.broadcasted_iota(jnp.int32, (full, outer), 1)).astype(jnp.float32).astype(jnp.bfloat16)
    wide = lax.broadcasted_iota(jnp.int32, (outer, full), 1) & (outer - 1)
    across = (wide == lax.broadcasted_iota(jnp.int32, (outer, full), 0)).astype(jnp.float32).astype(jnp.bfloat16)
    copies = jnp.dot(down, right, preferred_element_type=jnp.float32).astype(jnp.bfloat16)
    copies = jnp.dot(copies, across, preferred_element_type=jnp.float32)
    at = lax.broadcasted_iota(jnp.int32, (full, full), 0)
    of = lax.broadcasted_iota(jnp.int32, (full, full), 1)
    odd = (at >= 2 * outer) == ((of & outer) != 0)
    query = ((at & outer) != 0) == (of >= 2 * outer)
    return jnp.where(odd & query, copies, 0.0).astype(jnp.bfloat16)


def ring_kernel(
    size, count_all, queries_ref, train_ref, left_ref, right_ref, scores_ref,
    held, train, acc, flipped, mine, sums, raw, before, after,
    raw_sem, train_sem, send_sem, recv_sem, twin_send, twin_recv, sum_send, sum_recv,
):
    modules, inner, _ = left_ref.shape
    outer = right_ref.shape[1]
    half = inner // 2
    chips = size // 2
    rows = queries_ref.shape[1]
    width = inner * outer
    total = 2 * rows
    block = size * rows
    me = lax.axis_index("ex")
    place, core = me // 2, lax.rem(me, 2)
    twin = place * 2 + 1 - core
    snake = size == 16

    def place_of(at):
        if not snake:
            return at
        side = at // (chips // 2)
        return 2 * (at + side * (chips - 1 - 2 * at)) + side

    at = place
    if snake:
        side, high = lax.rem(place, 2), place // 2
        at = high + side * (chips - 1 - 2 * high)
    ahead = place_of(lax.rem(at + 1, chips)) * 2 + core
    behind = place_of(lax.rem(at + chips - 1, chips)) * 2 + core

    def part(index):
        return pl.ds(index * width, width)

    def raw_copy(index):
        return pltpu.make_async_copy(
            queries_ref.at[:, :, part(index)], raw.at[:, :, part(index)], raw_sem.at[index]
        )

    def train_copy(index):
        return pltpu.make_async_copy(
            train_ref.at[:, part(index)], train.at[:, part(index)], train_sem.at[index]
        )

    for index in range(modules):
        raw_copy(index).start()
    for index in range(modules):
        train_copy(index).start()

    barrier = pltpu.get_barrier_semaphore()

    @pl.loop(1, size)
    def _(shift):
        pl.semaphore_signal(
            barrier, inc=1, device_id={"ex": lax.rem(me + shift, size)},
            device_id_type=pl.DeviceIdType.MESH,
        )

    def source(way, step):
        return place_of(lax.rem(at + (chips - step if way == 0 else step), chips))

    def slot(way, step, whose, index):
        start = (source(way, step) * 2 + whose) * rows
        return held.at[way, pl.ds(pl.multiple_of(start, rows), rows), part(index)]

    def forward(way, step, index):
        view = slot(way, step, core, index)
        return pltpu.make_async_remote_copy(
            src_ref=view, dst_ref=view,
            send_sem=send_sem.at[way, index], recv_sem=recv_sem.at[way, step, index],
            device_id={"ex": ahead if way == 0 else behind},
            device_id_type=pl.DeviceIdType.MESH,
        )

    def share(way, step, index):
        view = slot(way, step, core, index)
        return pltpu.make_async_remote_copy(
            src_ref=view, dst_ref=view,
            send_sem=twin_send.at[way, index], recv_sem=twin_recv.at[way, step, index],
            device_id={"ex": twin}, device_id_type=pl.DeviceIdType.MESH,
        )

    def arrived(way, step, whose, index, sem):
        view = slot(way, step, whose, index)
        pltpu.make_async_copy(view, view, sem).wait()

    def condition(index):
        left = spread_left(left_ref[index])
        right = spread_right(right_ref[index])
        own = pl.ds(pl.multiple_of(me * rows, rows), rows)
        for pair in range(half):
            columns = pl.ds(index * width + pair * LANES, LANES)
            for way in range(2):
                before[pair * total + way * rows : pair * total + (way + 1) * rows, :] = raw[
                    way, :, columns
                ].astype(jnp.float32)

        group = 8

        @pl.loop(0, total, step=group)
        def _(first):
            low = lax.broadcasted_iota(jnp.int32, (half, LANES), 1) < outer
            stacks = []
            for query in range(0, group, 2):
                here = before[pl.ds(first + query, half, stride=total), :]
                there = before[pl.ds(first + query + 1, half, stride=total), :]
                even = jnp.where(low, here, pltpu.roll(there, outer, 1))
                odd = jnp.where(low, pltpu.roll(here, outer, 1), there)
                stacks.append(jnp.concatenate([even, odd], axis=0))
            stack = jnp.concatenate(stacks, axis=1).astype(jnp.bfloat16)
            halfway = jnp.dot(left, stack, preferred_element_type=jnp.float32).astype(jnp.bfloat16)
            sides = [
                jnp.concatenate(
                    [
                        halfway[:half, query * LANES : (query + 1) * LANES],
                        halfway[half:, query * LANES : (query + 1) * LANES],
                    ],
                    axis=1,
                )
                for query in range(group // 2)
            ]
            full = jnp.dot(jnp.concatenate(sides, axis=0), right, preferred_element_type=jnp.float32)
            for query in range(group):
                at_row, at_lane = query // 2 * half, query % 2 * LANES
                after[pl.ds(first + query, half, stride=total), :] = full[
                    at_row : at_row + half, at_lane : at_lane + LANES
                ]

        for pair in range(half):
            columns = pl.ds(index * width + pair * LANES, LANES)
            for way in range(2):
                held[way, own, columns] = after[
                    pair * total + way * rows : pair * total + (way + 1) * rows, :
                ].astype(jnp.bfloat16)

    def multiply(step, index):
        for way in range(2):
            arrived(way, step, 1 - core, index, twin_recv.at[way, step, index])
        pair = [
            held[way, pl.ds(pl.multiple_of(source(way, step) * total, total), total), part(index)]
            for way in range(2)
        ]
        product = lax.dot_general(
            train[:, part(index)], jnp.concatenate(pair, axis=0),
            (((1,), (1,)), ((), ())), preferred_element_type=jnp.float32,
        )
        if index == 0:
            acc[...] = product
        elif index < modules - 1:
            acc[...] += product
        else:
            turned = (acc[...] + product).T
            for way in range(2):
                start = way * block + source(way, step) * total
                flipped[pl.ds(pl.multiple_of(start, total), total), :] = turned[
                    way * total : (way + 1) * total
                ]

    for index in range(modules):
        raw_copy(index).wait()
        condition(index)
        if index == 0:
            pl.semaphore_wait(barrier, size - 1)
        for way in range(2):
            forward(way, 0, index).start()
            share(way, 0, index).start()

    for index in range(modules):
        train_copy(index).wait()
        multiply(0, index)

    def take(step, index, last):
        for way in range(2):
            arrived(way, step, core, index, recv_sem.at[way, step - 1, index])
            forward(way, step - 1, index).wait_send()
            if not last:
                forward(way, step, index).start()
            share(way, step - 1, index).wait_send()
            share(way, step, index).start()

    @pl.loop(1, chips - 1)
    def _(step):
        for index in range(modules):
            take(step, index, False)
            multiply(step, index)

    def finish(start):
        columns = flipped[pl.ds(start, LANES), :].T
        scores_ref[:, pl.ds(start, LANES)] = columns
        mine[:, pl.ds(start, LANES)] = jnp.sum(columns * columns, axis=0, keepdims=True)

    late = [
        way * (block // LANES) + source(way, chips - 1) * total // LANES for way in range(2)
    ]
    for index in range(modules):
        take(chips - 1, index, True)
        multiply(chips - 1, index)
        if index == 0:
            @pl.loop(0, 2 * block // LANES)
            def _(chunk):
                @pl.when((chunk != late[0]) & (chunk != late[1]))
                def _():
                    finish(pl.multiple_of(chunk * LANES, LANES))

    for way in range(2):
        finish(pl.multiple_of(late[way] * LANES, LANES))

    def tell(shift):
        return pltpu.make_async_remote_copy(
            src_ref=mine, dst_ref=sums.at[shift],
            send_sem=sum_send.at[shift], recv_sem=sum_recv.at[shift],
            device_id={"ex": lax.rem(me + shift, size)},
            device_id_type=pl.DeviceIdType.MESH,
        )

    @pl.loop(1, size)
    def _(shift):
        tell(shift).start()

    sums[0] = mine[...]
    for index in range(modules):
        for way in range(2):
            share(way, chips - 1, index).wait_send()

    @pl.loop(1, size)
    def _(shift):
        tell(shift).wait()

    inverse_rms = lax.rsqrt(jnp.sum(sums[...], axis=0) / count_all + 1e-06)
    scores_ref[...] = scores_ref[...] * inverse_rms


def on_device(train_grads, queries, left_factor, right_factor):
    size = lax.axis_size("ex")
    count, features = train_grads.shape
    blocks, rows, _ = queries.shape
    modules, inner, _ = left_factor.shape
    columns = blocks * size * rows
    chips = size // 2
    strip = (inner // 2 * 2 * rows, LANES)
    return pl.pallas_call(
        functools.partial(ring_kernel, size, count * size),
        out_shape=jax.ShapeDtypeStruct((count, columns), jnp.float32),
        in_specs=[pl.BlockSpec(memory_space=pl.ANY)] * 2 + [pl.BlockSpec(memory_space=pltpu.VMEM)] * 2,
        out_specs=pl.BlockSpec(memory_space=pltpu.VMEM),
        scratch_shapes=[
            pltpu.VMEM((2, size * rows, features), jnp.bfloat16),
            pltpu.VMEM((count, features), jnp.bfloat16),
            pltpu.VMEM((count, 4 * rows), jnp.float32),
            pltpu.VMEM((columns, count), jnp.float32),
            pltpu.VMEM((1, columns), jnp.float32),
            pltpu.VMEM((size, 1, columns), jnp.float32),
            pltpu.VMEM((2, rows, features), jnp.bfloat16),
            pltpu.VMEM(strip, jnp.float32),
            pltpu.VMEM(strip, jnp.float32),
            pltpu.SemaphoreType.DMA((modules,)),
            pltpu.SemaphoreType.DMA((modules,)),
            pltpu.SemaphoreType.DMA((2, modules)),
            pltpu.SemaphoreType.DMA((2, chips - 1, modules)),
            pltpu.SemaphoreType.DMA((2, modules)),
            pltpu.SemaphoreType.DMA((2, chips, modules)),
            pltpu.SemaphoreType.DMA((size,)),
            pltpu.SemaphoreType.DMA((size,)),
        ],
        compiler_params=pltpu.CompilerParams(
            collective_id=0, has_side_effects=True, vmem_limit_bytes=60 * 1024 * 1024
        ),
        cost_estimate=pl.CostEstimate(
            flops=2 * count * columns * features,
            bytes_accessed=2 * count * features + 4 * count * columns,
            transcendentals=0,
        ),
    )(queries, train_grads, left_factor, right_factor)


def solution(mesh):
    in_specs = (P(("grp", "ex"), None), P(None, ("grp", "ex"), None), P(), P())
    out_specs = P(("grp", "ex"), None)
    return jax.shard_map(
        on_device, mesh=mesh, in_specs=in_specs, out_specs=out_specs, check_vma=False
    )
```

```python
import functools

import jax
import jax.numpy as jnp
from jax import lax
from jax.experimental import pallas as pl
from jax.experimental.pallas import tpu as pltpu
from jax.sharding import PartitionSpec as P

LANES = 128


def spread_left(left):
    inner = left.shape[0]
    half = inner // 2
    at = lax.broadcasted_iota(jnp.int32, (inner, inner), 0)
    of = lax.broadcasted_iota(jnp.int32, (inner, inner), 1)
    move = (of == jnp.where(at < half, 2 * at, 2 * (at - half) + 1)).astype(jnp.float32).astype(jnp.bfloat16)
    back = (at == jnp.where(of < half, 2 * of, 2 * (of - half) + 1)).astype(jnp.float32).astype(jnp.bfloat16)
    rows_moved = jnp.dot(move, left, preferred_element_type=jnp.float32).astype(jnp.bfloat16)
    return jnp.dot(rows_moved, back, preferred_element_type=jnp.float32).astype(jnp.bfloat16)


def spread_right(right):
    outer = right.shape[0]
    full = 4 * outer
    tall = lax.broadcasted_iota(jnp.int32, (full, outer), 0) & (outer - 1)
    down = (tall == lax.broadcasted_iota(jnp.int32, (full, outer), 1)).astype(jnp.float32).astype(jnp.bfloat16)
    wide = lax.broadcasted_iota(jnp.int32, (outer, full), 1) & (outer - 1)
    across = (wide == lax.broadcasted_iota(jnp.int32, (outer, full), 0)).astype(jnp.float32).astype(jnp.bfloat16)
    copies = jnp.dot(down, right, preferred_element_type=jnp.float32).astype(jnp.bfloat16)
    copies = jnp.dot(copies, across, preferred_element_type=jnp.float32)
    at = lax.broadcasted_iota(jnp.int32, (full, full), 0)
    of = lax.broadcasted_iota(jnp.int32, (full, full), 1)
    odd = (at >= 2 * outer) == ((of & outer) != 0)
    query = ((at & outer) != 0) == (of >= 2 * outer)
    return jnp.where(odd & query, copies, 0.0).astype(jnp.bfloat16)


def ring_kernel(
    size, count_all, queries_ref, train_ref, left_ref, right_ref, scores_ref,
    held, train, acc, flipped, mine, sums, raw, before, after,
    raw_sem, train_sem, send_sem, recv_sem, twin_send, twin_recv, sum_send, sum_recv,
):
    modules, inner, _ = left_ref.shape
    outer = right_ref.shape[1]
    half = inner // 2
    chips = size // 2
    rows = queries_ref.shape[1]
    width = inner * outer
    total = 2 * rows
    block = size * rows
    me = lax.axis_index("ex")
    place, core = me // 2, lax.rem(me, 2)
    twin = place * 2 + 1 - core
    snake = size == 16

    def place_of(at):
        if not snake:
            return at
        side = at // (chips // 2)
        return 2 * (at + side * (chips - 1 - 2 * at)) + side

    at = place
    if snake:
        side, high = lax.rem(place, 2), place // 2
        at = high + side * (chips - 1 - 2 * high)
    ahead = place_of(lax.rem(at + 1, chips)) * 2 + core
    behind = place_of(lax.rem(at + chips - 1, chips)) * 2 + core

    def part(index):
        return pl.ds(index * width, width)

    def raw_copy(index):
        return pltpu.make_async_copy(
            queries_ref.at[:, :, part(index)], raw.at[:, :, part(index)], raw_sem.at[index]
        )

    def train_copy(index):
        return pltpu.make_async_copy(
            train_ref.at[:, part(index)], train.at[:, part(index)], train_sem.at[index]
        )

    for index in range(modules):
        raw_copy(index).start()
    for index in range(modules):
        train_copy(index).start()

    barrier = pltpu.get_barrier_semaphore()

    @pl.loop(1, size)
    def _(shift):
        pl.semaphore_signal(
            barrier, inc=1, device_id={"ex": lax.rem(me + shift, size)},
            device_id_type=pl.DeviceIdType.MESH,
        )

    def source(way, step):
        return place_of(lax.rem(at + (chips - step if way == 0 else step), chips))

    def slot(way, step, whose, index):
        start = (source(way, step) * 2 + whose) * rows
        return held.at[way, pl.ds(pl.multiple_of(start, rows), rows), part(index)]

    def forward(way, step, index):
        view = slot(way, step, core, index)
        return pltpu.make_async_remote_copy(
            src_ref=view, dst_ref=view,
            send_sem=send_sem.at[way, index], recv_sem=recv_sem.at[way, step, index],
            device_id={"ex": ahead if way == 0 else behind},
            device_id_type=pl.DeviceIdType.MESH,
        )

    def share(way, step, index):
        view = slot(way, step, core, index)
        return pltpu.make_async_remote_copy(
            src_ref=view, dst_ref=view,
            send_sem=twin_send.at[way, index], recv_sem=twin_recv.at[way, step, index],
            device_id={"ex": twin}, device_id_type=pl.DeviceIdType.MESH,
        )

    def arrived(way, step, whose, index, sem):
        view = slot(way, step, whose, index)
        pltpu.make_async_copy(view, view, sem).wait()

    def condition(index, way, left, right):
        own = pl.ds(pl.multiple_of(me * rows, rows), rows)
        for pair in range(half):
            columns = pl.ds(index * width + pair * LANES, LANES)
            before[pair * total + way * rows : pair * total + (way + 1) * rows, :] = raw[
                way, :, columns
            ].astype(jnp.float32)

        group = 8

        @pl.loop(way * rows, (way + 1) * rows, step=group)
        def _(first):
            low = lax.broadcasted_iota(jnp.int32, (half, LANES), 1) < outer
            stacks = []
            for query in range(0, group, 2):
                here = before[pl.ds(first + query, half, stride=total), :]
                there = before[pl.ds(first + query + 1, half, stride=total), :]
                even = jnp.where(low, here, pltpu.roll(there, outer, 1))
                odd = jnp.where(low, pltpu.roll(here, outer, 1), there)
                stacks.append(jnp.concatenate([even, odd], axis=0))
            stack = jnp.concatenate(stacks, axis=1).astype(jnp.bfloat16)
            halfway = jnp.dot(left, stack, preferred_element_type=jnp.float32).astype(jnp.bfloat16)
            sides = [
                jnp.concatenate(
                    [
                        halfway[:half, query * LANES : (query + 1) * LANES],
                        halfway[half:, query * LANES : (query + 1) * LANES],
                    ],
                    axis=1,
                )
                for query in range(group // 2)
            ]
            full = jnp.dot(jnp.concatenate(sides, axis=0), right, preferred_element_type=jnp.float32)
            for query in range(group):
                at_row, at_lane = query // 2 * half, query % 2 * LANES
                after[pl.ds(first + query, half, stride=total), :] = full[
                    at_row : at_row + half, at_lane : at_lane + LANES
                ]

        for pair in range(half):
            columns = pl.ds(index * width + pair * LANES, LANES)
            held[way, own, columns] = after[
                pair * total + way * rows : pair * total + (way + 1) * rows, :
            ].astype(jnp.bfloat16)

    def multiply(step, index):
        for way in range(2):
            arrived(way, step, 1 - core, index, twin_recv.at[way, step, index])
        pair = [
            held[way, pl.ds(pl.multiple_of(source(way, step) * total, total), total), part(index)]
            for way in range(2)
        ]
        product = lax.dot_general(
            train[:, part(index)], jnp.concatenate(pair, axis=0),
            (((1,), (1,)), ((), ())), preferred_element_type=jnp.float32,
        )
        if index == 0:
            acc[...] = product
        elif index < modules - 1:
            acc[...] += product
        else:
            turned = (acc[...] + product).T
            for way in range(2):
                start = way * block + source(way, step) * total
                flipped[pl.ds(pl.multiple_of(start, total), total), :] = turned[
                    way * total : (way + 1) * total
                ]

    for index in range(modules):
        raw_copy(index).wait()
        left = spread_left(left_ref[index])
        right = spread_right(right_ref[index])
        for way in range(2):
            condition(index, way, left, right)
            if index == 0 and way == 0:
                pl.semaphore_wait(barrier, size - 1)
            forward(way, 0, index).start()
            share(way, 0, index).start()

    for index in range(modules):
        train_copy(index).wait()
        multiply(0, index)

    def take(step, index, last):
        for way in range(2):
            arrived(way, step, core, index, recv_sem.at[way, step - 1, index])
            forward(way, step - 1, index).wait_send()
            if not last:
                forward(way, step, index).start()
            share(way, step - 1, index).wait_send()
            share(way, step, index).start()

    @pl.loop(1, chips - 1)
    def _(step):
        for index in range(modules):
            take(step, index, False)
            multiply(step, index)

    def finish(start):
        columns = flipped[pl.ds(start, LANES), :].T
        scores_ref[:, pl.ds(start, LANES)] = columns
        mine[:, pl.ds(start, LANES)] = jnp.sum(columns * columns, axis=0, keepdims=True)

    late = [
        way * (block // LANES) + source(way, chips - 1) * total // LANES for way in range(2)
    ]
    for index in range(modules):
        take(chips - 1, index, True)
        multiply(chips - 1, index)
        if index == 0:
            @pl.loop(0, 2 * block // LANES)
            def _(chunk):
                @pl.when((chunk != late[0]) & (chunk != late[1]))
                def _():
                    finish(pl.multiple_of(chunk * LANES, LANES))

    for way in range(2):
        finish(pl.multiple_of(late[way] * LANES, LANES))

    def tell(shift):
        return pltpu.make_async_remote_copy(
            src_ref=mine, dst_ref=sums.at[shift],
            send_sem=sum_send.at[shift], recv_sem=sum_recv.at[shift],
            device_id={"ex": lax.rem(me + shift, size)},
            device_id_type=pl.DeviceIdType.MESH,
        )

    @pl.loop(1, size)
    def _(shift):
        tell(shift).start()

    sums[0] = mine[...]
    for index in range(modules):
        for way in range(2):
            share(way, chips - 1, index).wait_send()

    @pl.loop(1, size)
    def _(shift):
        tell(shift).wait()

    inverse_rms = lax.rsqrt(jnp.sum(sums[...], axis=0) / count_all + 1e-06)
    scores_ref[...] = scores_ref[...] * inverse_rms


def on_device(train_grads, queries, left_factor, right_factor):
    size = lax.axis_size("ex")
    count, features = train_grads.shape
    blocks, rows, _ = queries.shape
    modules, inner, _ = left_factor.shape
    columns = blocks * size * rows
    chips = size // 2
    strip = (inner // 2 * 2 * rows, LANES)
    return pl.pallas_call(
        functools.partial(ring_kernel, size, count * size),
        out_shape=jax.ShapeDtypeStruct((count, columns), jnp.float32),
        in_specs=[pl.BlockSpec(memory_space=pl.ANY)] * 2 + [pl.BlockSpec(memory_space=pltpu.VMEM)] * 2,
        out_specs=pl.BlockSpec(memory_space=pltpu.VMEM),
        scratch_shapes=[
            pltpu.VMEM((2, size * rows, features), jnp.bfloat16),
            pltpu.VMEM((count, features), jnp.bfloat16),
            pltpu.VMEM((count, 4 * rows), jnp.float32),
            pltpu.VMEM((columns, count), jnp.float32),
            pltpu.VMEM((1, columns), jnp.float32),
            pltpu.VMEM((size, 1, columns), jnp.float32),
            pltpu.VMEM((2, rows, features), jnp.bfloat16),
            pltpu.VMEM(strip, jnp.float32),
            pltpu.VMEM(strip, jnp.float32),
            pltpu.SemaphoreType.DMA((modules,)),
            pltpu.SemaphoreType.DMA((modules,)),
            pltpu.SemaphoreType.DMA((2, modules)),
            pltpu.SemaphoreType.DMA((2, chips - 1, modules)),
            pltpu.SemaphoreType.DMA((2, modules)),
            pltpu.SemaphoreType.DMA((2, chips, modules)),
            pltpu.SemaphoreType.DMA((size,)),
            pltpu.SemaphoreType.DMA((size,)),
        ],
        compiler_params=pltpu.CompilerParams(
            collective_id=0, has_side_effects=True, vmem_limit_bytes=60 * 1024 * 1024
        ),
        cost_estimate=pl.CostEstimate(
            flops=2 * count * columns * features,
            bytes_accessed=2 * count * features + 4 * count * columns,
            transcendentals=0,
        ),
    )(queries, train_grads, left_factor, right_factor)


def solution(mesh):
    in_specs = (P(("grp", "ex"), None), P(None, ("grp", "ex"), None), P(), P())
    out_specs = P(("grp", "ex"), None)
    return jax.shard_map(
        on_device, mesh=mesh, in_specs=in_specs, out_specs=out_specs, check_vma=False
    )
```
